32 devices in a mesh: seq: 8 (over y, x, core), head: 4 (over z).
Axes of the slice: x: 2, y: 2, z: 4, core: 2. Of those that a mesh axis runs over, the one named last changes fastest.
Arguments:
- inputs: bfloat16 [16384, 2048], P('seq'), may hold values from -6 to 6
- w_qkv: bfloat16 [3, 2048, 2048], P(None, None, 'head'), may hold values from -0.125 to 0.125
- norm_gain: float32 [2048], P('head'), may hold values from 0.1 to 1.9
- w_out: bfloat16 [2048, 2048], P('head'), may hold values from -0.125 to 0.125
Outputs:
- mixed: bfloat16 [16384, 2048], P(('seq', 'head'))
The draws below stay inside these ranges and needn't reach their ends.
All inputs are finite; a program needn't handle non-finite values.
Results may differ from the reference program's by a relative error of at most 0.0067.
Values may be sent and summed in bfloat16 or wider, within the bound.
A program may use at most 128 MiB of HBM per device.

```python
import jax
import jax.numpy as jnp
from jax import lax

D = 2048
H = 16
DH = 128
BLK = 256
TOKENS = 16384
HD = 2048


def steps_of(stream_key, shape, shards, least, top_value):
    def one(dim, shards_of):
        steps = jax.random.uniform(jax.random.fold_in(jax.random.fold_in(stream_key, 6), dim), (shards_of,), jnp.float32, least / len(shards), top_value / len(shards))
        return jnp.repeat(jnp.exp(steps), shape[dim] // shards_of).reshape((-1,) + (1,) * (len(shape) - dim - 1))

    level = one(*shards[0])
    for cut in shards[1:]:
        level = level * one(*cut)
    return level


def noise(own_key, shape, width, limit, cuts=(), kind=jnp.bfloat16):
    array = width * jax.random.normal(own_key, shape, jnp.float32)
    if cuts:
        array = array * steps_of(own_key, shape, cuts, -0.22, 0.18)
    return jnp.clip(array, -limit, limit).astype(kind)


def setup_inputs(seed: int = 0) -> dict:
    seeds = jax.random.split(jax.random.key(seed), 5)
    inputs = noise(seeds[0], (TOKENS, D), 1.0, 6.0, ((0, 8),))
    w_qkv = noise(seeds[1], (3, D, HD), D ** -0.5, 0.125, ((2, 4),))
    norm_gain = jnp.clip(1.0 + 0.18 * jax.random.normal(seeds[2], (HD,), jnp.float32), 0.1, 1.9)
    w_out = noise(seeds[3], (HD, D), HD ** -0.5, 0.125, ((0, 4),))
    return dict(inputs=inputs, w_qkv=w_qkv, norm_gain=norm_gain, w_out=w_out)


def reference(inputs, w_qkv, norm_gain, w_out):
    hp = lax.Precision.HIGHEST
    q = jnp.dot(inputs, w_qkv[0], preferred_element_type=jnp.float32).astype(jnp.bfloat16)
    k = jnp.dot(inputs, w_qkv[1], preferred_element_type=jnp.float32).astype(jnp.bfloat16)
    v = jnp.dot(inputs, w_qkv[2], preferred_element_type=jnp.float32).astype(jnp.bfloat16)
    count = q.shape[0] // BLK

    def split(arr):
        return arr.reshape(count, BLK, H, DH).transpose(0, 2, 1, 3)
    lower = jnp.tril(jnp.ones((BLK, BLK), jnp.bool_))

    def advance(state, block):
        qb, kb, vb = block
        qf = qb.astype(jnp.float32)
        kf = kb.astype(jnp.float32)
        vf = vb.astype(jnp.float32)
        scores = jnp.einsum('hid,hjd->hij', qf, kf, precision=hp)
        scores = jnp.where(lower[None], scores, 0.0).astype(jnp.bfloat16)
        intra = jnp.einsum('hij,hjd->hid', scores.astype(jnp.float32), vf, precision=hp)
        inter = jnp.einsum('hid,hde->hie', qf, state, precision=hp)
        state = state + jnp.einsum('hjd,hje->hde', kf, vf, precision=hp)
        return (state, intra + inter)
    start = jnp.zeros((H, DH, DH), jnp.float32)
    final, attended = lax.scan(advance, start, (split(q), split(k), split(v)))
    mean_sq = lax.optimization_barrier(jnp.mean(attended * attended, axis=-1, keepdims=True))
    gain = norm_gain.reshape(H, 1, DH)
    normed = (attended / jnp.sqrt(mean_sq + 1e-06) * gain).astype(jnp.bfloat16)
    normed = normed.transpose(0, 2, 1, 3).reshape(count * BLK, H * DH)
    return jnp.dot(normed, w_out, preferred_element_type=jnp.float32).astype(jnp.bfloat16)
```

```python
import jax
import jax.numpy as jnp
from jax import lax
from jax.sharding import PartitionSpec as P

DH = 128
BLK = 256


def carried_in(value, axis):
    length, position = (lax.axis_size(axis), lax.axis_index(axis))
    everything = lax.all_gather(value, axis)
    earlier = (jnp.arange(length) < position).reshape((length,) + (1,) * value.ndim)
    return jnp.sum(jnp.where(earlier, everything, 0.0), axis=0)


def on_device(inputs, w_qkv, norm_gain, w_out):
    hp = lax.Precision.HIGHEST
    tokens_here = inputs.shape[0]
    feats = w_qkv.shape[2]
    heads = feats // DH
    count = tokens_here // BLK
    seqs, heads_axis = lax.axis_size("seq"), lax.axis_size("head")
    share = w_out.shape[0] // seqs
    mine = lax.dynamic_slice_in_dim(w_out, lax.axis_index("seq") * share, share, axis=0)
    w_all = lax.all_gather(mine, ("head", "seq"), axis=0, tiled=True)
    projected = jnp.einsum("td,pdc->ptc", inputs, w_qkv, preferred_element_type=jnp.float32).astype(
        jnp.bfloat16
    )

    def split(arr):
        return arr.reshape(count, BLK, heads, DH).transpose(0, 2, 1, 3)

    query = split(projected[0])
    keys = split(projected[1])
    values = split(projected[2])
    block_states = jnp.einsum("nhjd,nhje->nhde", keys, values, preferred_element_type=jnp.float32)
    totals = jnp.sum(block_states, axis=0)
    local_prefix = jnp.cumsum(block_states, axis=0) - block_states
    carried = carried_in(totals, "seq")
    before = carried[None] + local_prefix
    lower = jnp.tril(jnp.ones((BLK, BLK), jnp.bool_))
    scores = jnp.einsum("nhid,nhjd->nhij", query, keys, preferred_element_type=jnp.float32)
    scores = jnp.where(lower[None, None], scores, 0.0).astype(jnp.bfloat16)
    intra = jnp.einsum("nhij,nhjd->nhid", scores, values, preferred_element_type=jnp.float32)
    inter = jnp.einsum("nhid,nhde->nhie", query.astype(jnp.float32), before, precision=hp)
    attended = intra + inter
    mean_sq = jnp.mean(attended * attended, axis=-1, keepdims=True)
    gain = norm_gain.reshape(1, heads, 1, DH)
    normed = (attended / jnp.sqrt(mean_sq + 1e-06) * gain).astype(jnp.bfloat16)
    normed = normed.transpose(0, 2, 1, 3).reshape(tokens_here, feats)
    regrouped = lax.all_to_all(normed, "head", split_axis=0, concat_axis=1, tiled=True)
    mixed = jnp.dot(regrouped, w_all, preferred_element_type=jnp.float32)
    return mixed.astype(jnp.bfloat16)


def solution(mesh):
    return jax.shard_map(
        on_device,
        mesh=mesh,
        in_specs=(P("seq", None), P(None, None, "head"), P("head"), P("head", None)),
        out_specs=P(("seq", "head"), None),
        check_vma=False,
    )
```

```python
import functools

import jax
import jax.numpy as jnp
from jax import lax
from jax.experimental import pallas as pl
from jax.experimental.pallas import tpu as pltpu
from jax.sharding import PartitionSpec as P

DH = 128
BLK = 256
EPS = 1e-06
MESH = pl.DeviceIdType.MESH


def flipped(index, mask):
    out, bit = index, 1
    while bit <= mask:
        if mask & bit:
            out = out + bit * (1 - 2 * ((index // bit) % 2))
        bit *= 2
    return out


def destinations(me, count):
    if count & (count - 1):
        return [lax.rem(me + step, count) for step in range(1, count)] + [me]
    half = count // 2
    masks = list(range(half, count)) + list(range(1, half)) + [0]
    return [flipped(me, mask) for mask in masks]


def mix_kernel(
    seqs, groups, x_hbm, w_hbm, gain_ref, out_ref,
    x_ref, w_ref, q_ref, k_ref, v_ref, prefix, total, outgoing, arrived, ready,
    x_sem, w_sem, own_sem, state_send, state_recv, send_sem, recv_sem,
):
    me, z = lax.axis_index("seq"), lax.axis_index("head")
    tokens, feats = q_ref.shape
    heads = feats // DH
    piece = tokens // groups
    blocks = piece // BLK

    def x_copy(c):
        rows = pl.ds(c * piece, piece)
        return pltpu.make_async_copy(x_hbm.at[rows], x_ref.at[rows], x_sem.at[c])

    def w_copy(p):
        return pltpu.make_async_copy(w_hbm.at[p], w_ref.at[p], w_sem.at[p])

    w_copy(1).start()
    x_copy(0).start()
    w_copy(2).start()
    for c in range(1, groups):
        x_copy(c).start()
    w_copy(0).start()

    barrier = pltpu.get_barrier_semaphore()
    for k in range(seqs):
        @pl.when(k != me)
        def _():
            pl.semaphore_signal(barrier, inc=1, device_id=(k, z), device_id_type=MESH)
    for k in range(groups):
        @pl.when(k != z)
        def _():
            pl.semaphore_signal(barrier, inc=1, device_id=(me, k), device_id_type=MESH)

    total[...] = jnp.zeros_like(total)
    w_copy(1).wait()

    for c in range(groups):
        x_copy(c).wait()
        rows = pl.ds(c * piece, piece)
        k_ref[rows, :] = jnp.dot(
            x_ref[rows, :], w_ref[1], preferred_element_type=jnp.float32
        ).astype(jnp.bfloat16)
        if c == 0:
            w_copy(2).wait()
        v_ref[rows, :] = jnp.dot(
            x_ref[rows, :], w_ref[2], preferred_element_type=jnp.float32
        ).astype(jnp.bfloat16)
        for b in range(blocks):
            n = c * blocks + b
            block = pl.ds(n * BLK, BLK)
            for h in range(heads):
                cols = pl.ds(h * DH, DH)
                before = total[h]
                prefix[n, h] = before
                total[h] = before + lax.dot_general(
                    k_ref[block, cols], v_ref[block, cols],
                    (((0,), (0,)), ((), ())), preferred_element_type=jnp.float32,
                )

    outgoing[...] = total[...].astype(jnp.bfloat16)
    pl.semaphore_wait(barrier, seqs + groups - 2)

    def state_copy(source, target):
        return pltpu.make_async_remote_copy(
            src_ref=outgoing, dst_ref=arrived.at[source],
            send_sem=state_send.at[target], recv_sem=state_recv.at[source],
            device_id=(target, z), device_id_type=MESH,
        )

    for k in reversed(range(seqs)):
        @pl.when(k > me)
        def _():
            state_copy(me, k).start()

    w_copy(0).wait()
    for c in range(groups):
        rows = pl.ds(c * piece, piece)
        q_ref[rows, :] = jnp.dot(
            x_ref[rows, :], w_ref[0], preferred_element_type=jnp.float32
        ).astype(jnp.bfloat16)

    total[...] = jnp.zeros_like(total)
    for k in range(seqs):
        @pl.when(k < me)
        def _():
            state_copy(k, me).wait_recv()
            total[...] += arrived[k].astype(jnp.float32)

    lower = lax.broadcasted_iota(jnp.int32, (BLK, BLK), 0) >= lax.broadcasted_iota(
        jnp.int32, (BLK, BLK), 1
    )

    def attend(n, h):
        block, cols = pl.ds(n * BLK, BLK), pl.ds(h * DH, DH)
        q, v = q_ref[block, cols], v_ref[block, cols]
        scores = lax.dot_general(
            q, k_ref[block, cols], (((1,), (1,)), ((), ())), preferred_element_type=jnp.float32
        )
        scores = jnp.where(lower, scores, 0.0).astype(jnp.bfloat16)
        before = total[h] + prefix[n, h]
        high = before.astype(jnp.bfloat16)
        low = (before - high.astype(jnp.float32)).astype(jnp.bfloat16)
        attended = jnp.dot(scores, v, preferred_element_type=jnp.float32) + jnp.dot(
            jnp.concatenate([q, q], axis=1), jnp.concatenate([high, low], axis=0),
            preferred_element_type=jnp.float32,
        )
        mean_sq = jnp.mean(attended * attended, axis=-1, keepdims=True)
        return (attended * lax.rsqrt(mean_sq + EPS) * gain_ref[:, cols]).astype(jnp.bfloat16)

    def ready_copy(source, target):
        return pltpu.make_async_remote_copy(
            src_ref=ready.at[target],
            dst_ref=out_ref.at[:, pl.ds(source * feats, feats)],
            send_sem=send_sem.at[target], recv_sem=recv_sem.at[source],
            device_id=(me, target), device_id_type=MESH,
        )

    order = destinations(z, groups)
    for target in order:
        for b in range(blocks):
            for h in range(heads):
                ready[target, pl.ds(b * BLK, BLK), pl.ds(h * DH, DH)] = attend(
                    target * blocks + b, h
                )
        if target is not order[-1]:
            ready_copy(z, target).start()
    own = pltpu.make_async_copy(
        ready.at[z], out_ref.at[:, pl.ds(pl.multiple_of(z * feats, feats), feats)], own_sem
    )
    own.start()
    own.wait()
    for target in order[:-1]:
        ready_copy(target, target).wait_recv()
    for target in order[:-1]:
        ready_copy(z, target).wait_send()
    for k in range(seqs):
        @pl.when(k > me)
        def _():
            state_copy(me, k).wait_send()


def on_device(inputs, w_qkv, norm_gain, w_out):
    tokens, width = inputs.shape
    feats = w_qkv.shape[2]
    heads = feats // DH
    seqs, groups = lax.axis_size("seq"), lax.axis_size("head")
    share = w_out.shape[0] // seqs
    mine = lax.dynamic_slice_in_dim(w_out, lax.axis_index("seq") * share, share, axis=0)
    w_all = lax.all_gather(mine, ("head", "seq"), axis=0, tiled=True)
    piece = tokens // groups
    regrouped = pl.pallas_call(
        functools.partial(mix_kernel, seqs, groups),
        out_shape=jax.ShapeDtypeStruct((piece, groups * feats), jnp.bfloat16),
        in_specs=[
            pl.BlockSpec(memory_space=pl.ANY),
            pl.BlockSpec(memory_space=pl.ANY),
            pl.BlockSpec(memory_space=pltpu.VMEM),
        ],
        out_specs=pl.BlockSpec(memory_space=pl.ANY),
        scratch_shapes=[
            pltpu.VMEM((tokens, width), jnp.bfloat16),
            pltpu.VMEM(w_qkv.shape, jnp.bfloat16),
            pltpu.VMEM((tokens, feats), jnp.bfloat16),
            pltpu.VMEM((tokens, feats), jnp.bfloat16),
            pltpu.VMEM((tokens, feats), jnp.bfloat16),
            pltpu.VMEM((tokens // BLK, heads, DH, DH), jnp.float32),
            pltpu.VMEM((heads, DH, DH), jnp.float32),
            pltpu.VMEM((heads, DH, DH), jnp.bfloat16),
            pltpu.VMEM((seqs, heads, DH, DH), jnp.bfloat16),
            pltpu.VMEM((groups, piece, feats), jnp.bfloat16),
            pltpu.SemaphoreType.DMA((groups,)),
            pltpu.SemaphoreType.DMA((3,)),
            pltpu.SemaphoreType.DMA,
            pltpu.SemaphoreType.DMA((seqs,)),
            pltpu.SemaphoreType.DMA((seqs,)),
            pltpu.SemaphoreType.DMA((groups,)),
            pltpu.SemaphoreType.DMA((groups,)),
        ],
        compiler_params=pltpu.CompilerParams(
            collective_id=0, has_side_effects=True, vmem_limit_bytes=56 * 2**20
        ),
        cost_estimate=pl.CostEstimate(
            flops=2 * tokens * feats * (3 * width + 4 * BLK),
            bytes_accessed=2 * (tokens * width + 3 * width * feats) + 200 * 10**6,
            transcendentals=0,
        ),
    )(inputs, w_qkv, norm_gain.reshape(1, feats))
    return jnp.dot(regrouped, w_all, preferred_element_type=jnp.float32).astype(jnp.bfloat16)


def solution(mesh):
    return jax.shard_map(
        on_device,
        mesh=mesh,
        in_specs=(P("seq", None), P(None, None, "head"), P("head"), P("head", None)),
        out_specs=P(("seq", "head"), None),
        check_vma=False,
    )
```

```python
import functools

import jax
import jax.numpy as jnp
from jax import lax
from jax.experimental import pallas as pl
from jax.experimental.pallas import tpu as pltpu
from jax.sharding import PartitionSpec as P

DH = 128
BLK = 256
EPS = 1e-06
MESH = pl.DeviceIdType.MESH


def flipped(index, mask):
    out, bit = index, 1
    while bit <= mask:
        if mask & bit:
            out = out + bit * (1 - 2 * ((index // bit) % 2))
        bit *= 2
    return out


def destinations(me, count):
    if count & (count - 1):
        return [lax.rem(me + step, count) for step in range(1, count)] + [me]
    half = count // 2
    masks = list(range(half, count)) + list(range(1, half)) + [0]
    return [flipped(me, mask) for mask in masks]


def mix_kernel(
    seqs, groups, x_hbm, w_hbm, gain_ref, wo_hbm, out_hbm,
    x_ref, w_ref, q_ref, k_ref, v_ref, prefix, total, outgoing, arrived, ready,
    landed, wo_ref, acc, out_ref,
    x_sem, w_sem, own_sem, state_send, state_recv, send_sem, recv_sem,
    along_send, plane_send, pair_send, wo_recv, out_sem,
):
    me, z = lax.axis_index("seq"), lax.axis_index("head")
    tokens, feats = q_ref.shape
    heads = feats // DH
    piece = tokens // groups
    blocks = piece // BLK
    share = feats // seqs
    chips, chip, core = seqs // 2, me // 2, me % 2
    order = destinations(z, groups)
    others = destinations(chip, chips)[:-1]

    def wo_rows(group, seq):
        return pl.ds(pl.multiple_of(group * feats + seq * share, share), share)

    def own_share():
        return wo_hbm.at[pl.ds(pl.multiple_of(me * share, share), share)]

    def along_copy(source, target):
        return pltpu.make_async_remote_copy(
            src_ref=own_share(), dst_ref=wo_ref.at[wo_rows(source, me)],
            send_sem=along_send.at[target], recv_sem=wo_recv.at[source, me],
            device_id=(me, target), device_id_type=MESH,
        )

    def relay_copy(group, seq, target, send):
        return pltpu.make_async_remote_copy(
            src_ref=wo_ref.at[wo_rows(group, seq)], dst_ref=wo_ref.at[wo_rows(group, seq)],
            send_sem=send, recv_sem=wo_recv.at[group, seq],
            device_id=(target, z), device_id_type=MESH,
        )

    def plane_copy(group, other):
        return relay_copy(group, me, other * 2 + core, plane_send.at[group, other])

    def pair_copy(group, other):
        return relay_copy(group, other * 2 + core, chip * 2 + 1 - core, pair_send.at[group, other])

    def x_copy(c):
        rows = pl.ds(c * piece, piece)
        return pltpu.make_async_copy(x_hbm.at[rows], x_ref.at[rows], x_sem.at[c])

    def w_copy(p):
        return pltpu.make_async_copy(w_hbm.at[p], w_ref.at[p], w_sem.at[p])

    w_copy(1).start()
    x_copy(0).start()
    w_copy(2).start()
    for c in range(1, groups):
        x_copy(c).start()
    w_copy(0).start()
    own_wo = pltpu.make_async_copy(own_share(), wo_ref.at[wo_rows(z, me)], wo_recv.at[z, me])
    own_wo.start()

    barrier = pltpu.get_barrier_semaphore()
    for k in range(seqs):
        @pl.when(k != me)
        def _():
            pl.semaphore_signal(barrier, inc=1, device_id=(k, z), device_id_type=MESH)
    for k in range(groups):
        @pl.when(k != z)
        def _():
            pl.semaphore_signal(barrier, inc=1, device_id=(me, k), device_id_type=MESH)

    total[...] = jnp.zeros_like(total)
    pl.semaphore_wait(barrier, seqs + groups - 2)
    for target in order[:-1]:
        along_copy(z, target).start()
    own_wo.wait()
    for other in others:
        plane_copy(z, other).start()
    pair_copy(z, chip).start()
    w_copy(1).wait()

    for c in range(groups):
        x_copy(c).wait()
        rows = pl.ds(c * piece, piece)
        k_ref[rows, :] = jnp.dot(
            x_ref[rows, :], w_ref[1], preferred_element_type=jnp.float32
        ).astype(jnp.bfloat16)
        if c == 0:
            w_copy(2).wait()
        v_ref[rows, :] = jnp.dot(
            x_ref[rows, :], w_ref[2], preferred_element_type=jnp.float32
        ).astype(jnp.bfloat16)
        for b in range(blocks):
            n = c * blocks + b
            block = pl.ds(n * BLK, BLK)
            for h in range(heads):
                cols = pl.ds(h * DH, DH)
                before = total[h]
                prefix[n, h] = before
                total[h] = before + lax.dot_general(
                    k_ref[block, cols], v_ref[block, cols],
                    (((0,), (0,)), ((), ())), preferred_element_type=jnp.float32,
                )

    outgoing[...] = total[...].astype(jnp.bfloat16)

    def state_copy(source, target):
        return pltpu.make_async_remote_copy(
            src_ref=outgoing, dst_ref=arrived.at[source],
            send_sem=state_send.at[target], recv_sem=state_recv.at[source],
            device_id=(target, z), device_id_type=MESH,
        )

    for k in reversed(range(seqs)):
        @pl.when(k > me)
        def _():
            state_copy(me, k).start()

    w_copy(0).wait()
    for c in range(groups):
        rows = pl.ds(c * piece, piece)
        q_ref[rows, :] = jnp.dot(
            x_ref[rows, :], w_ref[0], preferred_element_type=jnp.float32
        ).astype(jnp.bfloat16)

    total[...] = jnp.zeros_like(total)
    for k in range(seqs):
        @pl.when(k < me)
        def _():
            state_copy(k, me).wait_recv()
            total[...] += arrived[k].astype(jnp.float32)

    for group in order[:-1]:
        along_copy(group, group).wait_recv()
        for other in others:
            plane_copy(group, other).start()
        pair_copy(group, chip).start()

    lower = lax.broadcasted_iota(jnp.int32, (BLK, BLK), 0) >= lax.broadcasted_iota(
        jnp.int32, (BLK, BLK), 1
    )

    def attend(n, h):
        block, cols = pl.ds(n * BLK, BLK), pl.ds(h * DH, DH)
        q, v = q_ref[block, cols], v_ref[block, cols]
        scores = lax.dot_general(
            q, k_ref[block, cols], (((1,), (1,)), ((), ())), preferred_element_type=jnp.float32
        )
        scores = jnp.where(lower, scores, 0.0).astype(jnp.bfloat16)
        before = total[h] + prefix[n, h]
        high = before.astype(jnp.bfloat16)
        low = (before - high.astype(jnp.float32)).astype(jnp.bfloat16)
        attended = jnp.dot(scores, v, preferred_element_type=jnp.float32) + jnp.dot(
            jnp.concatenate([q, q], axis=1), jnp.concatenate([high, low], axis=0),
            preferred_element_type=jnp.float32,
        )
        mean_sq = jnp.mean(attended * attended, axis=-1, keepdims=True)
        return (attended * lax.rsqrt(mean_sq + EPS) * gain_ref[:, cols]).astype(jnp.bfloat16)

    def ready_copy(source, target):
        return pltpu.make_async_remote_copy(
            src_ref=ready.at[target],
            dst_ref=landed.at[source],
            send_sem=send_sem.at[target], recv_sem=recv_sem.at[source],
            device_id=(me, target), device_id_type=MESH,
        )

    for target in order:
        for b in range(blocks):
            for h in range(heads):
                ready[target, pl.ds(b * BLK, BLK), pl.ds(h * DH, DH)] = attend(
                    target * blocks + b, h
                )
        if target is not order[-1]:
            ready_copy(z, target).start()

    relayed = [z] + order[:-1]
    for group in relayed:
        for other in others:
            relay_copy(group, other * 2 + core, me, plane_send.at[group, other]).wait_recv()
            pair_copy(group, other).start()

    columns = feats
    width = out_ref.shape[1]
    for step, group in enumerate(relayed):
        for other in others + [chip]:
            relay_copy(
                group, other * 2 + 1 - core, me, pair_send.at[group, other]
            ).wait_recv()
        if step > 0:
            ready_copy(group, group).wait_recv()
        source = ready if step == 0 else landed
        rows = pl.ds(pl.multiple_of(group * feats, feats), feats)
        for c in range(width // columns):
            cols = pl.ds(c * columns, columns)
            part = jnp.dot(source[group], wo_ref[rows, cols], preferred_element_type=jnp.float32)
            if step > 0:
                part += acc[:, cols]
            if step < groups - 1:
                acc[:, cols] = part
            else:
                out_ref[:, cols] = part.astype(jnp.bfloat16)
                pltpu.make_async_copy(
                    out_ref.at[:, cols], out_hbm.at[:, cols], out_sem.at[c]
                ).start()
    for c in range(width // columns):
        cols = pl.ds(c * columns, columns)
        pltpu.make_async_copy(out_ref.at[:, cols], out_hbm.at[:, cols], out_sem.at[c]).wait()

    for target in order[:-1]:
        ready_copy(z, target).wait_send()
        along_copy(z, target).wait_send()
    for group in relayed:
        for other in others:
            plane_copy(group, other).wait_send()
        for other in others + [chip]:
            pair_copy(group, other).wait_send()
    for k in range(seqs):
        @pl.when(k > me)
        def _():
            state_copy(me, k).wait_send()


def on_device(inputs, w_qkv, norm_gain, w_out):
    tokens, width = inputs.shape
    feats = w_qkv.shape[2]
    heads = feats // DH
    seqs, groups = lax.axis_size("seq"), lax.axis_size("head")
    piece = tokens // groups
    return pl.pallas_call(
        functools.partial(mix_kernel, seqs, groups),
        out_shape=jax.ShapeDtypeStruct((piece, w_out.shape[1]), jnp.bfloat16),
        in_specs=[
            pl.BlockSpec(memory_space=pl.ANY),
            pl.BlockSpec(memory_space=pl.ANY),
            pl.BlockSpec(memory_space=pltpu.VMEM),
            pl.BlockSpec(memory_space=pl.ANY),
        ],
        out_specs=pl.BlockSpec(memory_space=pl.ANY),
        scratch_shapes=[
            pltpu.VMEM((tokens, width), jnp.bfloat16),
            pltpu.VMEM(w_qkv.shape, jnp.bfloat16),
            pltpu.VMEM((tokens, feats), jnp.bfloat16),
            pltpu.VMEM((tokens, feats), jnp.bfloat16),
            pltpu.VMEM((tokens, feats), jnp.bfloat16),
            pltpu.VMEM((tokens // BLK, heads, DH, DH), jnp.float32),
            pltpu.VMEM((heads, DH, DH), jnp.float32),
            pltpu.VMEM((heads, DH, DH), jnp.bfloat16),
            pltpu.VMEM((seqs, heads, DH, DH), jnp.bfloat16),
            pltpu.VMEM((groups, piece, feats), jnp.bfloat16),
            pltpu.VMEM((groups, piece, feats), jnp.bfloat16),
            pltpu.VMEM((groups * feats, w_out.shape[1]), jnp.bfloat16),
            pltpu.VMEM((piece, w_out.shape[1]), jnp.float32),
            pltpu.VMEM((piece, w_out.shape[1]), jnp.bfloat16),
            pltpu.SemaphoreType.DMA((groups,)),
            pltpu.SemaphoreType.DMA((3,)),
            pltpu.SemaphoreType.DMA,
            pltpu.SemaphoreType.DMA((seqs,)),
            pltpu.SemaphoreType.DMA((seqs,)),
            pltpu.SemaphoreType.DMA((groups,)),
            pltpu.SemaphoreType.DMA((groups,)),
            pltpu.SemaphoreType.DMA((groups,)),
            pltpu.SemaphoreType.DMA((groups, seqs // 2)),
            pltpu.SemaphoreType.DMA((groups, seqs // 2)),
            pltpu.SemaphoreType.DMA((groups, seqs)),
            pltpu.SemaphoreType.DMA((w_out.shape[1] // feats,)),
        ],
        compiler_params=pltpu.CompilerParams(
            collective_id=0, has_side_effects=True, vmem_limit_bytes=56 * 2**20
        ),
        cost_estimate=pl.CostEstimate(
            flops=2 * tokens * feats * (3 * width + 4 * BLK),
            bytes_accessed=2 * (tokens * width + 3 * width * feats) + 200 * 10**6,
            transcendentals=0,
        ),
    )(inputs, w_qkv, norm_gain.reshape(1, feats), w_out)


def solution(mesh):
    return jax.shard_map(
        on_device,
        mesh=mesh,
        in_specs=(P("seq", None), P(None, None, "head"), P("head"), P("head", None)),
        out_specs=P(("seq", "head"), None),
        check_vma=False,
    )
```

```python
import functools

import jax
import jax.numpy as jnp
from jax import lax
from jax.experimental import pallas as pl
from jax.experimental.pallas import tpu as pltpu
from jax.sharding import PartitionSpec as P

DH = 128
BLK = 256
EPS = 1e-06
MESH = pl.DeviceIdType.MESH


def flipped(index, mask):
    out, bit = index, 1
    while bit <= mask:
        if mask & bit:
            out = out + bit * (1 - 2 * ((index // bit) % 2))
        bit *= 2
    return out


def destinations(me, count):
    if count & (count - 1):
        return [lax.rem(me + step, count) for step in range(1, count)] + [me]
    half = count // 2
    masks = list(range(half, count)) + list(range(1, half)) + [0]
    return [flipped(me, mask) for mask in masks]


def mix_kernel(
    seqs, groups, x_hbm, w_hbm, gain_ref, wo_hbm, out_hbm,
    x_ref, w_ref, q_ref, k_ref, v_ref, prefix, total, outgoing, arrived, ready,
    landed, wo_ref, acc, out_ref,
    x_sem, w_sem, own_sem, state_send, state_recv, send_sem, recv_sem,
    along_send, plane_send, pair_send, wo_recv, out_sem,
):
    me, z = lax.axis_index("seq"), lax.axis_index("head")
    tokens, feats = q_ref.shape
    heads = feats // DH
    piece = tokens // groups
    blocks = piece // BLK
    share = feats // seqs
    chips, chip, core = seqs // 2, me // 2, me % 2
    order = destinations(z, groups)
    others = destinations(chip, chips)[:-1]

    def wo_rows(group, seq):
        return pl.ds(pl.multiple_of(group * feats + seq * share, share), share)

    def own_share():
        return wo_hbm.at[pl.ds(pl.multiple_of(me * share, share), share)]

    def along_copy(mask, bit):
        group = flipped(z, mask)
        rows = wo_ref.at[wo_rows(group, me)]
        return pltpu.make_async_remote_copy(
            src_ref=rows if mask else own_share(), dst_ref=rows,
            send_sem=along_send.at[mask + bit], recv_sem=wo_recv.at[group, me],
            device_id=(me, flipped(z, bit)), device_id_type=MESH,
        )

    def along_wait(mask):
        relay_copy(flipped(z, mask), me, me, along_send.at[mask]).wait_recv()

    def spread(mask):
        group = flipped(z, mask)
        for other in others:
            plane_copy(group, other).start()
        pair_copy(group, chip).start()

    bits = [1 << b for b in reversed(range(groups.bit_length() - 1))]
    hops = [
        (mask, bit) for mask in range(groups) for bit in bits
        if mask == 0 or bit < (mask & -mask)
    ]

    def relay_copy(group, seq, target, send):
        return pltpu.make_async_remote_copy(
            src_ref=wo_ref.at[wo_rows(group, seq)], dst_ref=wo_ref.at[wo_rows(group, seq)],
            send_sem=send, recv_sem=wo_recv.at[group, seq],
            device_id=(target, z), device_id_type=MESH,
        )

    def plane_copy(group, other):
        return relay_copy(group, me, other * 2 + core, plane_send.at[group, other])

    def pair_copy(group, other):
        return relay_copy(group, other * 2 + core, chip * 2 + 1 - core, pair_send.at[group, other])

    def x_copy(c):
        rows = pl.ds(c * piece, piece)
        return pltpu.make_async_copy(x_hbm.at[rows], x_ref.at[rows], x_sem.at[c])

    def w_copy(p):
        return pltpu.make_async_copy(w_hbm.at[p], w_ref.at[p], w_sem.at[p])

    w_copy(1).start()
    x_copy(0).start()
    w_copy(2).start()
    for c in range(1, groups):
        x_copy(c).start()
    w_copy(0).start()
    own_wo = pltpu.make_async_copy(own_share(), wo_ref.at[wo_rows(z, me)], wo_recv.at[z, me])
    own_wo.start()

    barrier = pltpu.get_barrier_semaphore()
    for k in range(seqs):
        @pl.when(k != me)
        def _():
            pl.semaphore_signal(barrier, inc=1, device_id=(k, z), device_id_type=MESH)
    for k in range(groups):
        @pl.when(k != z)
        def _():
            pl.semaphore_signal(barrier, inc=1, device_id=(me, k), device_id_type=MESH)

    total[...] = jnp.zeros_like(total)
    pl.semaphore_wait(barrier, seqs + groups - 2)
    for bit in bits:
        along_copy(0, bit).start()
    own_wo.wait()
    spread(0)
    w_copy(1).wait()

    for c in range(groups):
        x_copy(c).wait()
        rows = pl.ds(c * piece, piece)
        k_ref[rows, :] = jnp.dot(
            x_ref[rows, :], w_ref[1], preferred_element_type=jnp.float32
        ).astype(jnp.bfloat16)
        if c == 0:
            w_copy(2).wait()
        v_ref[rows, :] = jnp.dot(
            x_ref[rows, :], w_ref[2], preferred_element_type=jnp.float32
        ).astype(jnp.bfloat16)
        for b in range(blocks):
            n = c * blocks + b
            block = pl.ds(n * BLK, BLK)
            for h in range(heads):
                cols = pl.ds(h * DH, DH)
                before = total[h]
                prefix[n, h] = before
                total[h] = before + lax.dot_general(
                    k_ref[block, cols], v_ref[block, cols],
                    (((0,), (0,)), ((), ())), preferred_element_type=jnp.float32,
                )

    outgoing[...] = total[...].astype(jnp.bfloat16)

    def state_copy(source, target):
        return pltpu.make_async_remote_copy(
            src_ref=outgoing, dst_ref=arrived.at[source],
            send_sem=state_send.at[target], recv_sem=state_recv.at[source],
            device_id=(target, z), device_id_type=MESH,
        )

    for k in reversed(range(seqs)):
        @pl.when(k > me)
        def _():
            state_copy(me, k).start()

    relays = []
    for mask, bit in hops:
        if mask:
            if mask not in relays:
                along_wait(mask)
                relays.append(mask)
            along_copy(mask, bit).start()
    w_copy(0).wait()
    for c in range(groups):
        rows = pl.ds(c * piece, piece)
        q_ref[rows, :] = jnp.dot(
            x_ref[rows, :], w_ref[0], preferred_element_type=jnp.float32
        ).astype(jnp.bfloat16)

    total[...] = jnp.zeros_like(total)
    for k in range(seqs):
        @pl.when(k < me)
        def _():
            state_copy(k, me).wait_recv()
            total[...] += arrived[k].astype(jnp.float32)

    late = [mask for mask in range(1, groups) if mask not in relays and mask not in bits]
    for mask in relays:
        spread(mask)
    for mask in bits:
        if mask not in relays:
            along_wait(mask)
            spread(mask)

    lower = lax.broadcasted_iota(jnp.int32, (BLK, BLK), 0) >= lax.broadcasted_iota(
        jnp.int32, (BLK, BLK), 1
    )

    def attend(n, h):
        block, cols = pl.ds(n * BLK, BLK), pl.ds(h * DH, DH)
        q, v = q_ref[block, cols], v_ref[block, cols]
        scores = lax.dot_general(
            q, k_ref[block, cols], (((1,), (1,)), ((), ())), preferred_element_type=jnp.float32
        )
        scores = jnp.where(lower, scores, 0.0).astype(jnp.bfloat16)
        before = total[h] + prefix[n, h]
        high = before.astype(jnp.bfloat16)
        low = (before - high.astype(jnp.float32)).astype(jnp.bfloat16)
        attended = jnp.dot(scores, v, preferred_element_type=jnp.float32) + jnp.dot(
            jnp.concatenate([q, q], axis=1), jnp.concatenate([high, low], axis=0),
            preferred_element_type=jnp.float32,
        )
        mean_sq = jnp.mean(attended * attended, axis=-1, keepdims=True)
        return (attended * lax.rsqrt(mean_sq + EPS) * gain_ref[:, cols]).astype(jnp.bfloat16)

    def ready_copy(source, target, b):
        rows = pl.ds(b * BLK, BLK)
        return pltpu.make_async_remote_copy(
            src_ref=ready.at[target, rows], dst_ref=landed.at[source, rows],
            send_sem=send_sem.at[target, b], recv_sem=recv_sem.at[source, b],
            device_id=(me, target), device_id_type=MESH,
        )

    for step, target in enumerate(order):
        for b in range(blocks):
            for h in range(heads):
                ready[target, pl.ds(b * BLK, BLK), pl.ds(h * DH, DH)] = attend(
                    target * blocks + b, h
                )
            if step < groups - 1:
                ready_copy(z, target, b).start()
        if step == 0:
            for mask in late:
                along_wait(mask)
                spread(mask)

    relayed = [z] + order[:-1]
    for group in relayed:
        for other in others:
            relay_copy(group, other * 2 + core, me, plane_send.at[group, other]).wait_recv()
            pair_copy(group, other).start()

    columns = feats
    width = out_ref.shape[1]
    for step, group in enumerate(relayed):
        for other in others + [chip]:
            relay_copy(
                group, other * 2 + 1 - core, me, pair_send.at[group, other]
            ).wait_recv()
        if step > 0:
            for b in range(blocks):
                ready_copy(group, group, b).wait_recv()
        source = ready if step == 0 else landed
        rows = pl.ds(pl.multiple_of(group * feats, feats), feats)
        for c in range(width // columns):
            cols = pl.ds(c * columns, columns)
            part = jnp.dot(source[group], wo_ref[rows, cols], preferred_element_type=jnp.float32)
            if step > 0:
                part += acc[:, cols]
            if step < groups - 1:
                acc[:, cols] = part
            else:
                out_ref[:, cols] = part.astype(jnp.bfloat16)
                pltpu.make_async_copy(
                    out_ref.at[:, cols], out_hbm.at[:, cols], out_sem.at[c]
                ).start()
    for c in range(width // columns):
        cols = pl.ds(c * columns, columns)
        pltpu.make_async_copy(out_ref.at[:, cols], out_hbm.at[:, cols], out_sem.at[c]).wait()

    for target in order[:-1]:
        for b in range(blocks):
            ready_copy(z, target, b).wait_send()
    for mask, bit in hops:
        along_copy(mask, bit).wait_send()
    for group in relayed:
        for other in others:
            plane_copy(group, other).wait_send()
        for other in others + [chip]:
            pair_copy(group, other).wait_send()
    for k in range(seqs):
        @pl.when(k > me)
        def _():
            state_copy(me, k).wait_send()


def on_device(inputs, w_qkv, norm_gain, w_out):
    tokens, width = inputs.shape
    feats = w_qkv.shape[2]
    heads = feats // DH
    seqs, groups = lax.axis_size("seq"), lax.axis_size("head")
    piece = tokens // groups
    return pl.pallas_call(
        functools.partial(mix_kernel, seqs, groups),
        out_shape=jax.ShapeDtypeStruct((piece, w_out.shape[1]), jnp.bfloat16),
        in_specs=[
            pl.BlockSpec(memory_space=pl.ANY),
            pl.BlockSpec(memory_space=pl.ANY),
            pl.BlockSpec(memory_space=pltpu.VMEM),
            pl.BlockSpec(memory_space=pl.ANY),
        ],
        out_specs=pl.BlockSpec(memory_space=pl.ANY),
        scratch_shapes=[
            pltpu.VMEM((tokens, width), jnp.bfloat16),
            pltpu.VMEM(w_qkv.shape, jnp.bfloat16),
            pltpu.VMEM((tokens, feats), jnp.bfloat16),
            pltpu.VMEM((tokens, feats), jnp.bfloat16),
            pltpu.VMEM((tokens, feats), jnp.bfloat16),
            pltpu.VMEM((tokens // BLK, heads, DH, DH), jnp.float32),
            pltpu.VMEM((heads, DH, DH), jnp.float32),
            pltpu.VMEM((heads, DH, DH), jnp.bfloat16),
            pltpu.VMEM((seqs, heads, DH, DH), jnp.bfloat16),
            pltpu.VMEM((groups, piece, feats), jnp.bfloat16),
            pltpu.VMEM((groups, piece, feats), jnp.bfloat16),
            pltpu.VMEM((groups * feats, w_out.shape[1]), jnp.bfloat16),
            pltpu.VMEM((piece, w_out.shape[1]), jnp.float32),
            pltpu.VMEM((piece, w_out.shape[1]), jnp.bfloat16),
            pltpu.SemaphoreType.DMA((groups,)),
            pltpu.SemaphoreType.DMA((3,)),
            pltpu.SemaphoreType.DMA,
            pltpu.SemaphoreType.DMA((seqs,)),
            pltpu.SemaphoreType.DMA((seqs,)),
            pltpu.SemaphoreType.DMA((groups, piece // BLK)),
            pltpu.SemaphoreType.DMA((groups, piece // BLK)),
            pltpu.SemaphoreType.DMA((groups,)),
            pltpu.SemaphoreType.DMA((groups, seqs // 2)),
            pltpu.SemaphoreType.DMA((groups, seqs // 2)),
            pltpu.SemaphoreType.DMA((groups, seqs)),
            pltpu.SemaphoreType.DMA((w_out.shape[1] // feats,)),
        ],
        compiler_params=pltpu.CompilerParams(
            collective_id=0, has_side_effects=True, vmem_limit_bytes=56 * 2**20
        ),
        cost_estimate=pl.CostEstimate(
            flops=2 * tokens * feats * (3 * width + 4 * BLK),
            bytes_accessed=2 * (tokens * width + 3 * width * feats) + 200 * 10**6,
            transcendentals=0,
        ),
    )(inputs, w_qkv, norm_gain.reshape(1, feats), w_out)


def solution(mesh):
    return jax.shard_map(
        on_device,
        mesh=mesh,
        in_specs=(P("seq", None), P(None, None, "head"), P("head"), P("head", None)),
        out_specs=P(("seq", "head"), None),
        check_vma=False,
    )
```
